32 devices in a mesh: outer: 4 (over z), inner: 8 (over y, x, core).
Axes of the slice: x: 2, y: 2, z: 4, core: 2. Of those that a mesh axis runs over, the one named last changes fastest.
Arguments:
- patches: bfloat16 [128, 128, 1024], P(('outer', 'inner')), may hold values from -6 to 6
- cotangent: bfloat16 [128, 128, 1024], P(('outer', 'inner')), may hold values from -0.28125 to 0.28125
- segment_ids: int32 [128, 128], P(('outer', 'inner')), may hold values from 0 to 7, never falling along the last dimension, each value on 1 to 64 neighbouring positions
- live_packs: int32 [32], P(('outer', 'inner')), may hold values from 1 to 4, as said below
- norm_gain: float32 [1024], replicated, may hold values from 0.25 to 1.75
- qkv_weight: bfloat16 [1024, 3072], P('inner'), may hold values from -0.1875 to 0.1875
- out_weight: bfloat16 [1024, 1024], P('inner'), may hold values from -0.1875 to 0.1875
- signs_qkv: int32 [3072], replicated, may hold values from 0 to 1
- signs_out: int32 [1024], replicated, may hold values from 0 to 1
Outputs:
- qkv_grad: float32 [1024, 3072], P('inner')
- out_grad: float32 [1024, 1024], P('inner')
- gain_grad: float32 [1024], replicated
The draws below stay inside these ranges and needn't reach their ends.
Inputs may be any that keep to these rules, and one draw needn't show every extreme that they name: `live_packs`: the live slots of a device are its first ones; in every draw some device has all 4 slots live.
All inputs are finite; a program needn't handle non-finite values.
Results may differ from the reference program's by a relative error of at most 0.03.
Values may be sent and summed in bfloat16 or wider, within the bound.
A program may use at most 64 MiB of HBM per device.

```python
import math
import jax
import jax.numpy as jnp
import numpy as np
from jax import lax

D = 1024
HEAD_DIM = 64
L = 128
PACKS_DEV = 4
PACKS = 128
N_OUTER = 4
N_INNER = 8


def draw_live_packs(key, part):
    device_count = N_OUTER * N_INNER
    picked = jax.random.randint(key, (device_count,), 1, PACKS_DEV + 1)
    loads = jnp.maximum(1, picked * picked // PACKS_DEV)
    busiest = jax.random.randint(jax.random.fold_in(key, 7), (), 0, device_count)
    loads = jnp.where(jnp.arange(device_count) == busiest, PACKS_DEV, loads)
    return loads.astype(jnp.int32)


def draw_qkv_weight(key, part):
    main_key = jax.random.fold_in(key, 11)
    whole = jax.random.truncated_normal(main_key, -5.0, 5.0, (D, 3 * D), jnp.float32) * D ** (-0.5)
    return whole.astype(jnp.bfloat16)


def draw_patches(key, part):
    main_key = jax.random.fold_in(key, 21)
    whole = jax.random.truncated_normal(main_key, -6.0, 6.0, (PACKS, L, D), jnp.float32)
    return whole.astype(jnp.bfloat16)


def with_ends(result, own_key, smallest, largest):
    place = [jax.random.randint(jax.random.fold_in(own_key, axis), (), 0, length) for axis, length in enumerate(result.shape)]
    widest = result.shape.index(max(result.shape))
    neighbour = place[:widest] + [(place[widest] + 1) % result.shape[widest]] + place[widest + 1:]
    return result.at[tuple(place)].set(smallest).at[tuple(neighbour)].set(largest)


def shard_levels(stream_key, dims, cuts, least, high):
    level = 1.0
    for axis_at, blocks in cuts:
        heights = jax.random.uniform(jax.random.fold_in(jax.random.fold_in(stream_key, 6), axis_at), (blocks,), jnp.float32, least / len(cuts), high / len(cuts))
        level = level * jnp.repeat(jnp.exp(heights), dims[axis_at] // blocks).reshape((-1,) + (1,) * (len(dims) - 1 - axis_at))
    return level


def profile(number_of, total, bound, skew):
    portions = [(1 << 20) // math.isqrt(rank ** skew) + 1 for rank in range(2, number_of + 1)]
    spare, holding = total - bound - (number_of - 1), [1] * (number_of - 1)
    while spare > 0:
        movable = [i for i in range(number_of - 1) if holding[i] < bound]
        mass, budget = sum([portions[i] for i in movable]), spare
        for i in movable:
            more = min(bound - holding[i], max(1, budget * portions[i] // mass), spare)
            holding[i] = holding[i] + more
            spare = spare - more
    return np.array([bound] + holding)


def ragged_sizes(key, amount, total, bound, slope):
    if amount == 2:
        one = jax.random.randint(key, (), max(1, total - bound), min(bound, total - 1) + 1)
        return jnp.stack([one, total - one])
    sizes = jnp.asarray(profile(amount, total, bound, slope), jnp.int32)
    couples = (amount - 1) // 2
    source_of, receiver = sizes[1:1 + 2 * couples:2], sizes[2:2 + 2 * couples:2]
    room = jnp.minimum(source_of - 1, bound - receiver)
    passed = jax.random.randint(jax.random.fold_in(key, 1), (couples,), 0, 1 << 20) % (room + 1)
    sizes = sizes.at[1:1 + 2 * couples:2].set(source_of - passed).at[2:2 + 2 * couples:2].set(receiver + passed)
    return sizes[jax.random.permutation(jax.random.fold_in(key, 2), amount)]


def gaussian(key, dims, width, bound, pieces=(), held_as=jnp.bfloat16):
    drawn = jax.random.normal(key, dims, jnp.float32) * width
    if len(pieces) > 0:
        drawn = shard_levels(key, dims, pieces, -0.22, 0.18) * drawn
    return jnp.clip(drawn, min=-bound, max=bound).astype(held_as)


def setup_inputs(seed: int = 0) -> dict:
    seeds = jax.random.split(jax.random.key(seed), 10)
    return {
        "patches": draw_patches(jax.random.fold_in(seeds[9], 71), 0),
        "cotangent": gaussian(seeds[1], (PACKS, L, D), (6 * (PACKS_DEV * L * N_OUTER * N_INNER) ** -0.5), 0.28125, ((0, 32),)),
        "segment_ids": jax.vmap(lambda own: jnp.searchsorted(jnp.cumsum(ragged_sizes(own, 8, L, L // 2, 0)), jnp.arange(L), side="right"))(jax.random.split(seeds[2], PACKS)).reshape((PACKS, L)).astype(jnp.int32),
        "live_packs": draw_live_packs(jax.random.fold_in(seeds[9], 71), 0),
        "norm_gain": jnp.clip(1.0 + 0.15 * jax.random.normal(seeds[4], (D,), jnp.float32), 0.25, 1.75),
        "qkv_weight": draw_qkv_weight(jax.random.fold_in(seeds[9], 71), 0),
        "out_weight": gaussian(seeds[6], (D, D), D ** -0.5, 0.1875, ((0, 8),)),
        "signs_qkv": with_ends(jax.random.randint(seeds[7], (3 * D,), 0, 2), jax.random.fold_in(seeds[7], 1), 0, 1).astype(jnp.int32),
        "signs_out": with_ends(jax.random.randint(seeds[8], (D,), 0, 2), jax.random.fold_in(seeds[8], 1), 0, 1).astype(jnp.int32),
    }


EPSILON = 1e-06
CLIP_RATIO = 2.0
BLOCK_WIDTH = 128
BLOCK_SCALE = 0.08838834764831845

def hadamard_table():
    indices = jnp.arange(BLOCK_WIDTH, dtype=jnp.int32)
    common = jnp.zeros((BLOCK_WIDTH, BLOCK_WIDTH), jnp.int32)
    for level in range(7):
        stride = 2 ** level
        common = common + indices[:, None] // stride % 2 * (indices[None, :] // stride % 2)
    return (1 - 2 * (common % 2)).astype(jnp.float32) * BLOCK_SCALE

def normalize(inputs, norm_gain):
    center = inputs - lax.optimization_barrier(jnp.mean(inputs, axis=-1, keepdims=True))
    spread = lax.optimization_barrier(jnp.mean(center * center, axis=-1, keepdims=True))
    return center * lax.rsqrt(spread + EPSILON) * norm_gain

def attend(projected, segment_ids):
    pack_count, pack_length, triple_width = projected.shape
    model_width = triple_width // 3
    head_count = model_width // HEAD_DIM
    split = projected.astype(jnp.float32).reshape(pack_count, pack_length, 3, head_count, HEAD_DIM)
    queries = split[:, :, 0]
    keys_all = split[:, :, 1]
    values_all = split[:, :, 2]
    scores = jnp.einsum('bqhd,bkhd->bhqk', queries, keys_all) * HEAD_DIM ** (-0.5)
    allowed = segment_ids[:, :, None] == segment_ids[:, None, :]
    scores = jnp.where(allowed[:, None], scores, -1e+30)
    top_score = lax.stop_gradient(lax.optimization_barrier(jnp.max(scores, axis=-1, keepdims=True)))
    exponent = jnp.exp(scores - top_score)
    probable = (exponent / lax.optimization_barrier(jnp.sum(exponent, axis=-1, keepdims=True))).astype(jnp.bfloat16)
    mixed_heads = jnp.einsum('bhqk,bkhd->bqhd', probable.astype(jnp.float32), values_all)
    return mixed_heads.reshape(pack_count, pack_length, model_width).astype(jnp.bfloat16)

def contract_rows(left_side, right_side):
    return lax.dot_general(left_side, right_side, (((0,), (0,)), ((), ())), preferred_element_type=jnp.float32)

def contract_cols(left_side, right_side):
    return lax.dot_general(left_side, right_side, (((1,), (1,)), ((), ())), preferred_element_type=jnp.float32)

def layer_backward(patches, cotangent, segment_ids, norm_gain, qkv_weight, out_weight):
    pack_count, pack_length, model_width = patches.shape
    inputs = patches.astype(jnp.float32)
    normed, norm_pullback = jax.vjp(normalize, inputs, norm_gain)
    flat_hidden = normed.astype(jnp.bfloat16).reshape(-1, model_width)
    projected = jnp.dot(flat_hidden, qkv_weight, preferred_element_type=jnp.float32).astype(jnp.bfloat16)
    projected = projected.reshape(pack_count, pack_length, 3 * model_width)

    def attend_pack(stacked):
        return attend(stacked, segment_ids)
    attended, attend_pullback = jax.vjp(attend_pack, projected)
    flat_cotangent = cotangent.reshape(-1, model_width)
    grad_attended = contract_cols(flat_cotangent, out_weight).astype(jnp.bfloat16)
    grad_projected = attend_pullback(grad_attended.reshape(attended.shape))[0]
    flat_grad = grad_projected.reshape(-1, 3 * model_width)
    grad_hidden = contract_cols(flat_grad, qkv_weight)
    gain_term = norm_pullback(grad_hidden.reshape(normed.shape))[1]
    return (flat_hidden, flat_grad, attended.reshape(-1, model_width), gain_term)

def sign_values(sign_bits):
    return (1 - 2 * sign_bits).astype(jnp.float32)

def rotate(matrix, sign_bits):
    signed = matrix * sign_values(sign_bits)
    blocks = signed.reshape(-1, BLOCK_WIDTH)
    return jnp.dot(blocks, hadamard_table(), precision=lax.Precision.HIGHEST).reshape(matrix.shape)

def clip_blocks(rotated):
    blocks = rotated.reshape(-1, BLOCK_WIDTH)
    clip_bound = CLIP_RATIO * jnp.sqrt(lax.optimization_barrier(jnp.mean(blocks * blocks, axis=-1, keepdims=True)) + EPSILON)
    return jnp.clip(blocks, -clip_bound, clip_bound).reshape(rotated.shape)

def decode(summed, sign_bits):
    blocks = summed.reshape(-1, BLOCK_WIDTH)
    turned = jnp.dot(blocks, hadamard_table(), precision=lax.Precision.HIGHEST).reshape(summed.shape)
    return turned * sign_values(sign_bits)

def reference(patches, cotangent, segment_ids, live_packs, norm_gain, qkv_weight, out_weight, signs_qkv, signs_out):
    model_width = patches.shape[-1]

    def by_device(array):
        return array.reshape((N_OUTER, N_INNER, PACKS_DEV) + array.shape[1:])
    live_grid = live_packs.reshape(N_OUTER, N_INNER)

    def device_step(running, inputs):
        sum_qkv, sum_out, sum_gain = running
        pack_inputs, pack_cotangent, pack_segments, live_count = inputs
        live_mask = (jnp.arange(PACKS_DEV, dtype=jnp.int32) < live_count).astype(jnp.bfloat16)
        masked = pack_cotangent * live_mask[:, None, None]
        hidden, grad_projected, attended, gain_term = layer_backward(pack_inputs, masked, pack_segments, norm_gain, qkv_weight, out_weight)
        term_qkv = contract_rows(hidden, grad_projected)
        term_out = contract_rows(attended, masked.reshape(-1, model_width))
        term_qkv = lax.optimization_barrier(term_qkv.astype(jnp.bfloat16)).astype(jnp.float32)
        term_out = lax.optimization_barrier(term_out.astype(jnp.bfloat16)).astype(jnp.float32)
        return ((sum_qkv + term_qkv, sum_out + term_out, sum_gain + gain_term), None)

    def group_step(running, inputs):
        total_qkv, total_out, total_gain = running
        initial = (jnp.zeros((model_width, 3 * model_width), jnp.float32), jnp.zeros((model_width, model_width), jnp.float32), jnp.zeros((model_width,), jnp.float32))
        group_qkv, group_out, group_gain = lax.scan(device_step, initial, inputs)[0]
        total_qkv = total_qkv + clip_blocks(rotate(group_qkv, signs_qkv))
        total_out = total_out + clip_blocks(rotate(group_out, signs_out))
        return ((total_qkv, total_out, total_gain + group_gain), None)
    initial = (jnp.zeros((model_width, 3 * model_width), jnp.float32), jnp.zeros((model_width, model_width), jnp.float32), jnp.zeros((model_width,), jnp.float32))
    inputs = (by_device(patches), by_device(cotangent), by_device(segment_ids), live_grid)
    total_qkv, total_out, total_gain = lax.scan(group_step, initial, inputs)[0]
    return (decode(total_qkv, signs_qkv), decode(total_out, signs_out), total_gain)
```

```python
import functools

import jax
import jax.numpy as jnp
from jax import lax
from jax.experimental import pallas as pl
from jax.experimental.pallas import tpu as pltpu
from jax.sharding import PartitionSpec as P

HEAD_DIM = 64
EPSILON = 1e-06
CLIP_RATIO = 2.0
BLOCK = 128
BLOCK_SCALE = 0.08838834764831845
GROUP = 256
F32 = jnp.float32
BF16 = jnp.bfloat16
MESH = pl.DeviceIdType.MESH


def dot_nn(a, b):
    return lax.dot_general(a, b, (((1,), (0,)), ((), ())), preferred_element_type=F32)


def dot_nt(a, b):
    return lax.dot_general(a, b, (((1,), (1,)), ((), ())), preferred_element_type=F32)


def dot_tn(a, b):
    return lax.dot_general(a, b, (((0,), (0,)), ((), ())), preferred_element_type=F32)


def hadamard():
    rows = lax.broadcasted_iota(jnp.int32, (BLOCK, BLOCK), 0)
    cols = lax.broadcasted_iota(jnp.int32, (BLOCK, BLOCK), 1)
    common = rows & cols
    total = jnp.zeros_like(common)
    for level in range(7):
        total = total + ((common >> level) & 1)
    return (1 - 2 * (total & 1)).astype(F32).astype(BF16)


def turn(block, table):
    high = block.astype(BF16)
    low = (block - high.astype(F32)).astype(BF16)
    return (dot_nn(high, table) + dot_nn(low, table)) * BLOCK_SCALE


class Plan:
    def __init__(self, n_outer, n_inner, packs, length, width, rows):
        self.no, self.n = n_outer, n_inner
        self.bits = n_inner.bit_length() - 1
        self.packs, self.length, self.width, self.rows = packs, length, width, rows
        self.total = packs * length
        self.groups = width // GROUP
        self.share = rows // n_outer
        self.wire = BF16 if self.share % 16 == 0 else F32
        self.chunks = self.groups + 1
        self.cols = [3 * GROUP] * self.groups + [width]
        upper = list(range(self.bits - 1))
        self.orders = [upper[::-1], upper]
        per_gather = 2 * self.bits
        per_scatter = 1 + 2 * (self.bits - 1)
        per_outer = 2 * (self.no - 1)
        self.messages = (
            self.chunks * (per_gather + per_scatter + per_outer) + (self.no - 1) + self.bits
        )


def kernel(plan, x_ref, cot_ref, live_ref, bias_ref, gain_ref, wq_ref, wo_ref, sq_ref, so_ref,
           oq_ref, oo_ref, og_ref, *scratch):
    names = list(scratch)

    def take(count):
        got = names[:count]
        del names[:count]
        return got

    send_sem, recv_sem, hid, hid_t, cot, proj, gatt, att, att_t, gproj, gacc, gpart, gall = take(13)
    ch = plan.chunks
    weights, grads, from_twin, sums = take(ch), take(ch), take(ch), take(ch)
    clipped, from_outer, decoded = take(ch), take(ch), take(ch)
    steps = plan.bits - 1
    got_half = [[take(steps) for _ in range(2)] for _ in range(ch)]
    sum_half = [[take(steps - 1) for _ in range(2)] for _ in range(ch)]

    outer, inner = lax.axis_index("outer"), lax.axis_index("inner")
    bits, rows, length, no = plan.bits, plan.rows, plan.length, plan.no
    half = rows // 2
    stride = [2 ** (bits - 1 - b) for b in range(bits)]
    mine = [lax.rem(inner // stride[b], 2) for b in range(bits)]
    partner = [inner + (1 - 2 * mine[b]) * stride[b] for b in range(bits)]
    counter = [0]

    barrier = pltpu.get_barrier_semaphore()
    for b in range(bits):
        pl.semaphore_signal(barrier, inc=1, device_id={"inner": partner[b]}, device_id_type=MESH)
    for j in range(1, no):
        pl.semaphore_signal(
            barrier, inc=1, device_id={"outer": lax.rem(outer + j, no)}, device_id_type=MESH
        )

    def message(src, dst, where):
        at = counter[0]
        counter[0] += 1
        return pltpu.make_async_remote_copy(
            src_ref=src, dst_ref=dst, send_sem=send_sem.at[at], recv_sem=recv_sem.at[at],
            device_id=where, device_id_type=MESH,
        )

    started = []

    def launch(messages):
        for one in messages:
            one.start()
            started.append(one)

    def arrive(messages):
        for one in messages:
            one.wait_recv()

    gathers = []
    for k in range(ch):
        levels = []
        for s in range(bits):
            level = []
            for h in range(2):
                order = plan.orders[h] + [bits - 1]
                spot = tuple(
                    slice(None) if b in order[:s] else mine[b] for b in range(bits)
                ) + (pl.ds(h * half, half),)
                ref = weights[k].at[spot]
                level.append(message(ref, ref, {"inner": partner[order[s]]}))
            levels.append(level)
        gathers.append(levels)

    def gather(k, s):
        if s > 0:
            arrive(gathers[k][s - 1])
        launch(gathers[k][s])

    own = tuple(mine)
    out = plan.groups
    weights[out][own] = wo_ref[...]
    for g in range(plan.groups):
        for part in range(3):
            at = part * plan.width + g * GROUP
            weights[g][own + (slice(None), pl.ds(part * GROUP, GROUP))] = wq_ref[:, at:at + GROUP]
    pl.semaphore_wait(barrier, bits + no - 1)

    gather_order = [out] + list(range(plan.groups))
    gather(out, 0)
    gather(0, 0)
    gather(1, 0)

    def norm_pack(p):
        at = pl.ds(pl.multiple_of(p * length, length), length)
        inputs = x_ref[at, :].astype(F32)
        center = inputs - jnp.mean(inputs, axis=-1, keepdims=True)
        spread = jnp.mean(center * center, axis=-1, keepdims=True)
        value = center * lax.rsqrt(spread + EPSILON) * gain_ref[...]
        hid[at, :] = value.astype(BF16)
        hid_t[:, at] = value.T.astype(BF16)
        cot[at, :] = (cot_ref[at, :].astype(F32) * live_ref[p][0:1, 0:1]).astype(BF16)

    pl.loop(0, plan.packs // 2)(norm_pack)
    gather(out, 1)
    gather(0, 1)
    pl.loop(plan.packs // 2, plan.packs)(norm_pack)
    gather(2, 0)
    gather(out, 2)
    gather(1, 1)
    gather(0, 2)
    arrive(gathers[out][bits - 1]) if bits == 3 else None

    table = hadamard()

    pending = []
    if bits != 3:
        for k in (out, 0):
            for s in range(3, bits):
                pending.append((k, s))
    for k in range(1, plan.groups):
        for s in range(bits):
            if (k, s) not in ((1, 0), (1, 1), (2, 0)):
                pending.append((k, s))

    def gather_upto(k):
        while any(entry[0] == k for entry in pending):
            gather(*pending.pop(0))

    if bits != 3:
        gather_upto(out)
        gather_upto(0)
        arrive(gathers[out][bits - 1])

    taken = bits - (GROUP // rows).bit_length() + 1

    def grad_att(g):
        spot = tuple((g >> (taken - 1 - b)) & 1 for b in range(taken))
        block = weights[out][spot].reshape(GROUP, plan.width)
        gatt[:, g * GROUP:(g + 1) * GROUP] = dot_nt(cot[...], block).astype(BF16)

    for g in range(plan.groups):
        grad_att(g)

    def project(g):
        arrive(gathers[g][bits - 1])
        for part in range(3):
            cols = pl.ds(part * GROUP, GROUP)
            block = weights[g][(slice(None),) * (bits + 1) + (cols,)]
            proj[:, cols] = dot_nn(hid[...], block.reshape(plan.width, GROUP)).astype(BF16)

    lane = lax.broadcasted_iota(jnp.int32, (length, BLOCK), 1)
    first = lane < HEAD_DIM

    def stack(value):
        zero = jnp.zeros_like(value)
        return jnp.concatenate([jnp.where(first, value, zero), jnp.where(first, zero, value)], 0)

    def pick(value):
        return jnp.where(first, value[:length], value[length:])

    def attend(g):
        def one(p):
            at = pl.ds(pl.multiple_of(p * length, length), length)
            bias = bias_ref[p]
            bias = jnp.concatenate([bias, bias], 0)
            for j in range(GROUP // BLOCK):
                cols = [pl.ds(part * GROUP + j * BLOCK, BLOCK) for part in range(3)]
                query, key, value = (proj[at, c] for c in cols)
                spot = g * GROUP + j * BLOCK
                queries = stack(query)
                scores = dot_nt(queries, key) * (HEAD_DIM ** -0.5) + bias
                power = jnp.exp(scores - jnp.max(scores, axis=-1, keepdims=True))
                prob = power / jnp.sum(power, axis=-1, keepdims=True)
                rounded = prob.astype(BF16)
                att[at, pl.ds(j * BLOCK, BLOCK)] = pick(dot_nn(rounded, value)).astype(BF16)
                grads_out = stack(gatt[at, spot:spot + BLOCK])
                grad_prob = dot_nt(grads_out, value).astype(BF16).astype(F32)
                inside = jnp.sum(grad_prob * prob, axis=-1, keepdims=True)
                grad_score = (prob * (grad_prob - inside) * (HEAD_DIM ** -0.5)).astype(BF16)
                gproj[at, cols[0]] = pick(dot_nn(grad_score, key)).astype(BF16)
                gproj[at, cols[1]] = dot_tn(grad_score, queries).astype(BF16)
                gproj[at, cols[2]] = dot_tn(rounded, grads_out).astype(BF16)

        pl.loop(0, plan.packs)(one)
        att_t[g * GROUP:(g + 1) * GROUP, :] = att[...].T

    def block_spot(i):
        return tuple((i >> (bits - 1 - b)) & 1 for b in range(bits))

    def weight_grad(k, left, right):
        tall = max(rows, GROUP)
        per = tall // rows
        for i in range(0, plan.n, per):
            product = dot_nn(left[i * rows:i * rows + tall, :], right[...]).astype(BF16)
            for e in range(per):
                grads[k][block_spot(i + e)] = product[e * rows:(e + 1) * rows]

    last = bits - 1
    live = {}

    def add(a, b):
        return a.astype(F32) + b.astype(F32)

    def stage_twin(k):
        spot = (slice(None),) * last
        msg = message(grads[k].at[spot + (1 - mine[last],)], from_twin[k], {"inner": partner[last]})
        launch([msg])
        live[k] = [msg]

    def stage_half(k, s):
        arrive(live[k])
        messages = []
        if s == 0:
            sums[k][...] = add(
                grads[k][(slice(None),) * last + (mine[last],)], from_twin[k][...]
            ).astype(BF16)
        finals = []
        for h in range(2):
            order = plan.orders[h][::-1]
            if s == 0:
                source, remaining = sums[k], list(range(last))
                tail = (pl.ds(h * half, half),)
            else:
                remaining = [b for b in range(last) if b not in order[:s - 1]]
                before = sums[k] if s == 1 else sum_half[k][h][s - 2]
                tail = (pl.ds(h * half, half),) if s == 1 else ()
                spot = tuple(
                    mine[b] if b == order[s - 1] else slice(None) for b in remaining
                ) + tail
                value = add(before[spot], got_half[k][h][s - 1][...])
                remaining = [b for b in remaining if b != order[s - 1]]
                if s == steps:
                    finals.append(value)
                    continue
                sum_half[k][h][s - 1][...] = value.astype(BF16)
                source, tail = sum_half[k][h][s - 1], ()
            spot = tuple(
                1 - mine[b] if b == order[s] else slice(None) for b in remaining
            ) + tail
            messages.append(message(
                source.at[spot], got_half[k][h][s], {"inner": partner[order[s]]}
            ))
        if s < steps:
            launch(messages)
            live[k] = messages
            return
        stage_clip(k, finals)

    def signs_at(k, b):
        if k == out:
            at, ref = b * BLOCK, so_ref
        else:
            per = GROUP // BLOCK
            at, ref = (b // per) * plan.width + k * GROUP + (b % per) * BLOCK, sq_ref
        return at, (1 - 2 * ref[:, at:at + BLOCK]).astype(F32)

    def stage_clip(k, finals):
        whole = jnp.concatenate(finals, 0)
        partial = None
        for b in range(plan.cols[k] // BLOCK):
            block = whole[:, b * BLOCK:(b + 1) * BLOCK]
            at, signs = signs_at(k, b)
            if k != out:
                term = block * wq_ref[:, at:at + BLOCK].astype(F32)
                partial = term if partial is None else partial + term
            value = turn(block * signs, table)
            bound = CLIP_RATIO * jnp.sqrt(
                jnp.mean(value * value, axis=-1, keepdims=True) + EPSILON
            )
            value = jnp.clip(value, -bound, bound)
            clipped[k][:, :, b * BLOCK:(b + 1) * BLOCK] = value.reshape(
                no, plan.share, BLOCK
            ).astype(plan.wire)
        if k != out:
            gacc[...] = partial if k == 0 else gacc[...] + partial
        messages = []
        for j in range(1, no):
            there = lax.rem(outer + j, no)
            messages.append(message(
                clipped[k].at[there], from_outer[k].at[j - 1], {"outer": there}
            ))
        launch(messages)
        live[k] = messages

    def stage_decode(k):
        arrive(live[k])
        total = clipped[k][outer].astype(F32)
        for j in range(1, no):
            total = total + from_outer[k][j - 1].astype(F32)
        for b in range(plan.cols[k] // BLOCK):
            signs = signs_at(k, b)[1]
            value = turn(total[:, b * BLOCK:(b + 1) * BLOCK], table) * signs
            decoded[k][outer, :, b * BLOCK:(b + 1) * BLOCK] = value.astype(plan.wire)
        messages = []
        for j in range(1, no):
            ref = decoded[k].at[outer]
            messages.append(message(ref, ref, {"outer": lax.rem(outer + j, no)}))
        launch(messages)
        live[k] = messages

    def stage_store(k):
        arrive(live[k])
        for part in range(1 if k == out else 3):
            wide = plan.width if k == out else GROUP
            value = decoded[k][:, :, part * wide:(part + 1) * wide].astype(F32)
            value = value.reshape(rows, wide)
            if k == out:
                oo_ref[...] = value
            else:
                at = part * plan.width + k * GROUP
                oq_ref[:, at:at + GROUP] = value

    def stages(k):
        todo = [functools.partial(stage_half, k, s) for s in range(steps + 1)]
        return todo + [functools.partial(stage_decode, k), functools.partial(stage_store, k)]

    queues = []

    def advance():
        for queue in queues:
            if queue:
                queue.pop(0)()

    for g in range(plan.groups):
        gather_upto(g)
        project(g)
        if g + 1 < plan.groups:
            while pending and pending[0][0] <= g + 1:
                gather(*pending.pop(0))
        advance()
        attend(g)
        if pending:
            gather(*pending.pop(0))
        advance()
        weight_grad(g, hid_t, gproj)
        stage_twin(g)
        queues.append(stages(g))
        if pending:
            gather(*pending.pop(0))
        advance() if g > 0 else None

    weight_grad(out, att_t, cot)
    stage_twin(out)
    queues.append(stages(out))
    while len(queues[out - 1]) > 2:
        advance()

    ones = jnp.ones((8, BLOCK), F32)
    gpart[outer] = lax.dot_general(
        ones, gacc[...], (((1,), (1,)), ((), ())), precision=lax.Precision.HIGHEST,
        preferred_element_type=F32,
    )
    gain_messages = []
    for j in range(1, no):
        ref = gpart.at[outer]
        gain_messages.append(message(ref, ref, {"outer": lax.rem(outer + j, no)}))
    launch(gain_messages)
    advance()
    arrive(gain_messages)
    total = gpart[0]
    for j in range(1, no):
        total = total + gpart[j]
    gall[own] = total
    for b in range(bits):
        spot = tuple(slice(None) if e < b else mine[e] for e in range(bits))
        ref = gall.at[spot]
        step = message(ref, ref, {"inner": partner[b]})
        launch([step])
        if b < 2:
            advance()
        arrive([step])
    for i in range(plan.n):
        og_ref[i] = gall[block_spot(i)]
    while any(queues):
        advance()
    for one in started:
        one.wait_send()


def on_device(plan, patches, cotangent, segment_ids, live_packs, norm_gain, qkv_weight, out_weight,
              signs_qkv, signs_out):
    width, rows, no = plan.width, plan.rows, plan.no
    flat = (plan.total, width)
    live = (jnp.arange(plan.packs, dtype=jnp.int32) < live_packs[0]).astype(F32)
    live = jnp.broadcast_to(live[:, None, None], (plan.packs, 8, BLOCK))
    allowed = segment_ids[:, :, None] == segment_ids[:, None, :]
    bias = jnp.where(allowed, 0.0, -1e30).astype(F32)
    two = (2,) * plan.bits
    vmem = pltpu.VMEM
    scratch = [
        pltpu.SemaphoreType.DMA((plan.messages,)),
        pltpu.SemaphoreType.DMA((plan.messages,)),
        vmem(flat, BF16),
        vmem(flat[::-1], BF16),
        vmem(flat, BF16),
        vmem((plan.total, 3 * GROUP), BF16),
        vmem(flat, BF16),
        vmem((plan.total, GROUP), BF16),
        vmem(flat[::-1], BF16),
        vmem((plan.total, 3 * GROUP), BF16),
        vmem((rows, BLOCK), F32),
        vmem((no, 8, rows), F32),
        vmem(two + (8, rows), F32),
    ]
    for shape, kind in (
        (two + (rows,), BF16), (two + (rows,), BF16), (two[1:] + (rows,), BF16),
        (two[1:] + (rows,), BF16), ((no, plan.share), plan.wire),
        ((no - 1, plan.share), plan.wire), ((no, plan.share), plan.wire),
    ):
        scratch += [vmem(shape + (cols,), kind) for cols in plan.cols]
    steps = plan.bits - 1
    for count in (steps, steps - 1):
        for cols in plan.cols:
            for _ in range(2):
                for s in range(count):
                    scratch.append(vmem((2,) * (steps - 1 - s) + (rows // 2, cols), BF16))
    qkv_grad, out_grad, gain = pl.pallas_call(
        functools.partial(kernel, plan),
        out_shape=(
            jax.ShapeDtypeStruct((rows, 3 * width), F32),
            jax.ShapeDtypeStruct((rows, width), F32),
            jax.ShapeDtypeStruct((plan.n, 8, rows), F32),
        ),
        in_specs=[pl.BlockSpec(memory_space=pltpu.VMEM)] * 9,
        out_specs=[pl.BlockSpec(memory_space=pltpu.VMEM)] * 3,
        scratch_shapes=scratch,
        compiler_params=pltpu.CompilerParams(
            collective_id=0, has_side_effects=True, vmem_limit_bytes=58 * 2**20
        ),
    )(
        patches.reshape(flat), cotangent.reshape(flat), live, bias, norm_gain[None], qkv_weight,
        out_weight, signs_qkv[None], signs_out[None],
    )
    return qkv_grad, out_grad, gain[:, 0].reshape(width) / norm_gain


def solution(mesh):
    def device(patches, cotangent, segment_ids, live_packs, norm_gain, qkv_weight, *others):
        packs, length, width = patches.shape
        plan = Plan(
            mesh.shape["outer"], mesh.shape["inner"], packs, length, width, qkv_weight.shape[0]
        )
        return on_device(
            plan, patches, cotangent, segment_ids, live_packs, norm_gain, qkv_weight, *others
        )

    return jax.shard_map(
        device,
        mesh=mesh,
        in_specs=(
            P(("outer", "inner"), None, None),
            P(("outer", "inner"), None, None),
            P(("outer", "inner"), None),
            P(("outer", "inner")),
            P(),
            P("inner", None),
            P("inner", None),
            P(),
            P(),
        ),
        out_specs=(P("inner", None), P("inner", None), P()),
        check_vma=False,
    )
```

```python
import functools

import jax
import jax.numpy as jnp
from jax import lax
from jax.experimental import pallas as pl
from jax.experimental.pallas import tpu as pltpu
from jax.sharding import PartitionSpec as P

HEAD_DIM = 64
EPSILON = 1e-06
CLIP_RATIO = 2.0
BLOCK = 128
BLOCK_SCALE = 0.08838834764831845
GROUP = 256
F32 = jnp.float32
BF16 = jnp.bfloat16
MESH = pl.DeviceIdType.MESH


def dot_nn(a, b):
    return lax.dot_general(a, b, (((1,), (0,)), ((), ())), preferred_element_type=F32)


def dot_nt(a, b):
    return lax.dot_general(a, b, (((1,), (1,)), ((), ())), preferred_element_type=F32)


def dot_tn(a, b):
    return lax.dot_general(a, b, (((0,), (0,)), ((), ())), preferred_element_type=F32)


def hadamard():
    rows = lax.broadcasted_iota(jnp.int32, (BLOCK, BLOCK), 0)
    cols = lax.broadcasted_iota(jnp.int32, (BLOCK, BLOCK), 1)
    common = rows & cols
    total = jnp.zeros_like(common)
    for level in range(7):
        total = total + ((common >> level) & 1)
    return (1 - 2 * (total & 1)).astype(F32).astype(BF16)


def turn(block, table):
    high = block.astype(BF16)
    low = (block - high.astype(F32)).astype(BF16)
    return (dot_nn(high, table) + dot_nn(low, table)) * BLOCK_SCALE


class Plan:
    def __init__(self, n_outer, n_inner, packs, length, width, rows):
        self.no, self.n = n_outer, n_inner
        self.bits = n_inner.bit_length() - 1
        self.packs, self.length, self.width, self.rows = packs, length, width, rows
        self.total = packs * length
        self.groups = width // GROUP
        self.share = rows // n_outer
        self.wire = BF16 if self.share % 16 == 0 else F32
        self.chunks = self.groups + 1
        self.cols = [3 * GROUP] * self.groups + [width]
        upper = list(range(self.bits - 1))
        self.orders = [upper[::-1], upper]
        per_gather = 2 * self.bits
        per_scatter = 1 + 2 * (self.bits - 1)
        per_outer = 2 * (self.no - 1)
        self.messages = (
            self.chunks * (per_gather + per_scatter + per_outer) + (self.no - 1) + self.bits
        )


def kernel(plan, x_ref, cot_ref, live_ref, bias_ref, gain_ref, wq_ref, wo_ref, sq_ref, so_ref,
           oq_ref, oo_ref, og_ref, *scratch):
    names = list(scratch)

    def take(count):
        got = names[:count]
        del names[:count]
        return got

    send_sem, recv_sem, hid, hid_t, cot, proj, gatt, att_t, gproj, gacc, gpart, gall = take(12)
    ch = plan.chunks
    weights, grads, from_twin, sums = take(ch), take(ch), take(ch), take(ch)
    clipped, from_outer, decoded = take(ch), take(ch), take(ch)
    steps = plan.bits - 1
    got_half = [[take(steps) for _ in range(2)] for _ in range(ch)]
    sum_half = [[take(steps - 1) for _ in range(2)] for _ in range(ch)]

    outer, inner = lax.axis_index("outer"), lax.axis_index("inner")
    bits, rows, length, no = plan.bits, plan.rows, plan.length, plan.no
    half = rows // 2
    stride = [2 ** (bits - 1 - b) for b in range(bits)]
    mine = [lax.rem(inner // stride[b], 2) for b in range(bits)]
    partner = [inner + (1 - 2 * mine[b]) * stride[b] for b in range(bits)]
    counter = [0]

    barrier = pltpu.get_barrier_semaphore()
    for b in range(bits):
        pl.semaphore_signal(barrier, inc=1, device_id={"inner": partner[b]}, device_id_type=MESH)
    for j in range(1, no):
        pl.semaphore_signal(
            barrier, inc=1, device_id={"outer": lax.rem(outer + j, no)}, device_id_type=MESH
        )

    def message(src, dst, where):
        at = counter[0]
        counter[0] += 1
        return pltpu.make_async_remote_copy(
            src_ref=src, dst_ref=dst, send_sem=send_sem.at[at], recv_sem=recv_sem.at[at],
            device_id=where, device_id_type=MESH,
        )

    started = []

    def launch(messages):
        for one in messages:
            one.start()
            started.append(one)

    def arrive(messages):
        for one in messages:
            one.wait_recv()

    gathers = []
    for k in range(ch):
        levels = []
        for s in range(bits):
            level = []
            for h in range(2):
                order = plan.orders[h] + [bits - 1]
                spot = tuple(
                    slice(None) if b in order[:s] else mine[b] for b in range(bits)
                ) + (pl.ds(h * half, half),)
                ref = weights[k].at[spot]
                level.append(message(ref, ref, {"inner": partner[order[s]]}))
            levels.append(level)
        gathers.append(levels)

    def gather(k, s):
        if s > 0:
            arrive(gathers[k][s - 1])
        launch(gathers[k][s])

    own = tuple(mine)
    out = plan.groups
    weights[out][own] = wo_ref[...]
    for g in range(plan.groups):
        for part in range(3):
            at = part * plan.width + g * GROUP
            weights[g][own + (slice(None), pl.ds(part * GROUP, GROUP))] = wq_ref[:, at:at + GROUP]
    pl.semaphore_wait(barrier, bits + no - 1)

    gather_order = [out] + list(range(plan.groups))
    gather(out, 0)
    gather(0, 0)
    gather(1, 0)

    def norm_pack(p):
        at = pl.ds(pl.multiple_of(p * length, length), length)
        inputs = x_ref[at, :].astype(F32)
        center = inputs - jnp.mean(inputs, axis=-1, keepdims=True)
        spread = jnp.mean(center * center, axis=-1, keepdims=True)
        value = center * lax.rsqrt(spread + EPSILON) * gain_ref[...]
        hid[at, :] = value.astype(BF16)
        hid_t[:, at] = value.T.astype(BF16)
        cot[at, :] = (cot_ref[at, :].astype(F32) * live_ref[p][0:1, 0:1]).astype(BF16)

    pl.loop(0, plan.packs // 2)(norm_pack)
    gather(out, 1)
    gather(0, 1)
    pl.loop(plan.packs // 2, plan.packs)(norm_pack)
    gather(2, 0)
    gather(out, 2)
    gather(1, 1)
    gather(0, 2)
    arrive(gathers[out][bits - 1]) if bits == 3 else None

    table = hadamard()

    pending = []
    if bits != 3:
        for k in (out, 0):
            for s in range(3, bits):
                pending.append((k, s))
    for k in range(1, plan.groups):
        for s in range(bits):
            if (k, s) not in ((1, 0), (1, 1), (2, 0)):
                pending.append((k, s))

    def gather_upto(k):
        while any(entry[0] == k for entry in pending):
            gather(*pending.pop(0))

    if bits != 3:
        gather_upto(out)
        gather_upto(0)
        arrive(gathers[out][bits - 1])

    taken = bits - (GROUP // rows).bit_length() + 1

    def grad_att(g):
        spot = tuple((g >> (taken - 1 - b)) & 1 for b in range(taken))
        block = weights[out][spot].reshape(GROUP, plan.width)
        gatt[:, g * GROUP:(g + 1) * GROUP] = dot_nt(cot[...], block).astype(BF16)

    for g in range(plan.groups):
        grad_att(g)

    def project(g):
        arrive(gathers[g][bits - 1])
        for part in range(3):
            cols = pl.ds(part * GROUP, GROUP)
            block = weights[g][(slice(None),) * (bits + 1) + (cols,)]
            proj[:, cols] = dot_nn(hid[...], block.reshape(plan.width, GROUP)).astype(BF16)

    lane = lax.broadcasted_iota(jnp.int32, (length, BLOCK), 1)
    first = lane < HEAD_DIM

    def stack(value):
        zero = jnp.zeros_like(value)
        return jnp.concatenate([jnp.where(first, value, zero), jnp.where(first, zero, value)], 0)

    paired = 2 if plan.packs % 2 == 0 else 1

    def attend(g):
        def one(p, j):
            at = pl.ds(pl.multiple_of(p * length, length), length)
            bias = bias_ref[p]
            bias = jnp.concatenate([bias, bias], 1)
            cols = [pl.ds(part * GROUP + j * BLOCK, BLOCK) for part in range(3)]
            query, key, value = (proj[at, c] for c in cols)
            spot = g * GROUP + j * BLOCK
            queries = stack(query)
            scores = dot_nt(key, queries) * (HEAD_DIM ** -0.5) + bias
            power = jnp.exp(scores - jnp.max(scores, axis=0, keepdims=True))
            prob = power * (1.0 / jnp.sum(power, axis=0, keepdims=True))
            rounded = prob.astype(BF16)
            mixed = dot_tn(value, rounded).astype(BF16)
            att_t[spot:spot + HEAD_DIM, at] = mixed[:HEAD_DIM, :length]
            att_t[spot + HEAD_DIM:spot + BLOCK, at] = mixed[HEAD_DIM:, length:]
            grads_out = stack(gatt[at, spot:spot + BLOCK])
            grad_prob = dot_nt(value, grads_out).astype(BF16).astype(F32)
            inside = jnp.sum(grad_prob * prob, axis=0, keepdims=True)
            grad_score = (prob * (grad_prob - inside) * (HEAD_DIM ** -0.5)).astype(BF16)
            turned = dot_tn(key, grad_score)
            turned = jnp.concatenate([turned[:HEAD_DIM, :length], turned[HEAD_DIM:, length:]], 0)
            gproj[at, cols[0]] = turned.T.astype(BF16)
            gproj[at, cols[1]] = dot_nn(grad_score, queries).astype(BF16)
            gproj[at, cols[2]] = dot_nn(rounded, grads_out).astype(BF16)

        @pl.loop(0, plan.packs // paired)
        def _(step):
            for e in range(paired):
                for j in range(GROUP // BLOCK):
                    one(step * paired + e, j)

    def block_spot(i):
        return tuple((i >> (bits - 1 - b)) & 1 for b in range(bits))

    def weight_grad(k, left, right):
        tall = max(rows, GROUP)
        per = tall // rows
        for i in range(0, plan.n, per):
            product = dot_nn(left[i * rows:i * rows + tall, :], right[...]).astype(BF16)
            for e in range(per):
                grads[k][block_spot(i + e)] = product[e * rows:(e + 1) * rows]

    last = bits - 1
    live = {}

    def add(a, b):
        return a.astype(F32) + b.astype(F32)

    def stage_twin(k):
        spot = (slice(None),) * last
        msg = message(grads[k].at[spot + (1 - mine[last],)], from_twin[k], {"inner": partner[last]})
        launch([msg])
        live[k] = [msg]

    def stage_half(k, s):
        arrive(live[k])
        messages = []
        if s == 0:
            sums[k][...] = add(
                grads[k][(slice(None),) * last + (mine[last],)], from_twin[k][...]
            ).astype(BF16)
        finals = []
        for h in range(2):
            order = plan.orders[h][::-1]
            if s == 0:
                source, remaining = sums[k], list(range(last))
                tail = (pl.ds(h * half, half),)
            else:
                remaining = [b for b in range(last) if b not in order[:s - 1]]
                before = sums[k] if s == 1 else sum_half[k][h][s - 2]
                tail = (pl.ds(h * half, half),) if s == 1 else ()
                spot = tuple(
                    mine[b] if b == order[s - 1] else slice(None) for b in remaining
                ) + tail
                value = add(before[spot], got_half[k][h][s - 1][...])
                remaining = [b for b in remaining if b != order[s - 1]]
                if s == steps:
                    finals.append(value)
                    continue
                sum_half[k][h][s - 1][...] = value.astype(BF16)
                source, tail = sum_half[k][h][s - 1], ()
            spot = tuple(
                1 - mine[b] if b == order[s] else slice(None) for b in remaining
            ) + tail
            messages.append(message(
                source.at[spot], got_half[k][h][s], {"inner": partner[order[s]]}
            ))
        if s < steps:
            launch(messages)
            live[k] = messages
            return
        stage_clip(k, finals)

    def signs_at(k, b):
        if k == out:
            at, ref = b * BLOCK, so_ref
        else:
            per = GROUP // BLOCK
            at, ref = (b // per) * plan.width + k * GROUP + (b % per) * BLOCK, sq_ref
        return at, (1 - 2 * ref[:, at:at + BLOCK]).astype(F32)

    def stage_clip(k, finals):
        whole = jnp.concatenate(finals, 0)
        partial = None
        for b in range(plan.cols[k] // BLOCK):
            block = whole[:, b * BLOCK:(b + 1) * BLOCK]
            at, signs = signs_at(k, b)
            if k != out:
                term = block * wq_ref[:, at:at + BLOCK].astype(F32)
                partial = term if partial is None else partial + term
            value = turn(block * signs, table)
            bound = CLIP_RATIO * jnp.sqrt(
                jnp.mean(value * value, axis=-1, keepdims=True) + EPSILON
            )
            value = jnp.clip(value, -bound, bound)
            clipped[k][:, :, b * BLOCK:(b + 1) * BLOCK] = value.reshape(
                no, plan.share, BLOCK
            ).astype(plan.wire)
        if k != out:
            gacc[...] = partial if k == 0 else gacc[...] + partial
        messages = []
        for j in range(1, no):
            there = lax.rem(outer + j, no)
            messages.append(message(
                clipped[k].at[there], from_outer[k].at[j - 1], {"outer": there}
            ))
        launch(messages)
        live[k] = messages

    def stage_decode(k):
        arrive(live[k])
        total = clipped[k][outer].astype(F32)
        for j in range(1, no):
            total = total + from_outer[k][j - 1].astype(F32)
        for b in range(plan.cols[k] // BLOCK):
            signs = signs_at(k, b)[1]
            value = turn(total[:, b * BLOCK:(b + 1) * BLOCK], table) * signs
            decoded[k][outer, :, b * BLOCK:(b + 1) * BLOCK] = value.astype(plan.wire)
        messages = []
        for j in range(1, no):
            ref = decoded[k].at[outer]
            messages.append(message(ref, ref, {"outer": lax.rem(outer + j, no)}))
        launch(messages)
        live[k] = messages

    def stage_store(k):
        arrive(live[k])
        for part in range(1 if k == out else 3):
            wide = plan.width if k == out else GROUP
            value = decoded[k][:, :, part * wide:(part + 1) * wide].astype(F32)
            value = value.reshape(rows, wide)
            if k == out:
                oo_ref[...] = value
            else:
                at = part * plan.width + k * GROUP
                oq_ref[:, at:at + GROUP] = value

    def stages(k):
        todo = [functools.partial(stage_half, k, s) for s in range(steps + 1)]
        return todo + [functools.partial(stage_decode, k), functools.partial(stage_store, k)]

    queues = []

    def advance():
        for queue in queues:
            if queue:
                queue.pop(0)()

    for g in range(plan.groups):
        gather_upto(g)
        project(g)
        if g + 1 < plan.groups:
            while pending and pending[0][0] <= g + 1:
                gather(*pending.pop(0))
        advance()
        attend(g)
        if pending:
            gather(*pending.pop(0))
        advance()
        weight_grad(g, hid_t, gproj)
        stage_twin(g)
        queues.append(stages(g))
        if pending:
            gather(*pending.pop(0))
        advance() if g > 0 else None

    weight_grad(out, att_t, cot)
    stage_twin(out)
    queues.append(stages(out))
    while len(queues[out - 1]) > 2:
        advance()

    ones = jnp.ones((8, BLOCK), F32)
    gpart[outer] = lax.dot_general(
        ones, gacc[...], (((1,), (1,)), ((), ())), precision=lax.Precision.HIGHEST,
        preferred_element_type=F32,
    )
    gain_messages = []
    for j in range(1, no):
        ref = gpart.at[outer]
        gain_messages.append(message(ref, ref, {"outer": lax.rem(outer + j, no)}))
    launch(gain_messages)
    advance()
    arrive(gain_messages)
    total = gpart[0]
    for j in range(1, no):
        total = total + gpart[j]
    gall[own] = total
    for b in range(bits):
        spot = tuple(slice(None) if e < b else mine[e] for e in range(bits))
        ref = gall.at[spot]
        step = message(ref, ref, {"inner": partner[b]})
        launch([step])
        if b < 2:
            advance()
        arrive([step])
    for i in range(plan.n):
        og_ref[i] = gall[block_spot(i)]
    while any(queues):
        advance()
    for one in started:
        one.wait_send()


def on_device(plan, patches, cotangent, segment_ids, live_packs, norm_gain, qkv_weight, out_weight,
              signs_qkv, signs_out):
    width, rows, no = plan.width, plan.rows, plan.no
    flat = (plan.total, width)
    live = (jnp.arange(plan.packs, dtype=jnp.int32) < live_packs[0]).astype(F32)
    live = jnp.broadcast_to(live[:, None, None], (plan.packs, 8, BLOCK))
    allowed = segment_ids[:, :, None] == segment_ids[:, None, :]
    bias = jnp.where(allowed, 0.0, -1e30).astype(F32)
    two = (2,) * plan.bits
    vmem = pltpu.VMEM
    scratch = [
        pltpu.SemaphoreType.DMA((plan.messages,)),
        pltpu.SemaphoreType.DMA((plan.messages,)),
        vmem(flat, BF16),
        vmem(flat[::-1], BF16),
        vmem(flat, BF16),
        vmem((plan.total, 3 * GROUP), BF16),
        vmem(flat, BF16),
        vmem(flat[::-1], BF16),
        vmem((plan.total, 3 * GROUP), BF16),
        vmem((rows, BLOCK), F32),
        vmem((no, 8, rows), F32),
        vmem(two + (8, rows), F32),
    ]
    for shape, kind in (
        (two + (rows,), BF16), (two + (rows,), BF16), (two[1:] + (rows,), BF16),
        (two[1:] + (rows,), BF16), ((no, plan.share), plan.wire),
        ((no - 1, plan.share), plan.wire), ((no, plan.share), plan.wire),
    ):
        scratch += [vmem(shape + (cols,), kind) for cols in plan.cols]
    steps = plan.bits - 1
    for count in (steps, steps - 1):
        for cols in plan.cols:
            for _ in range(2):
                for s in range(count):
                    scratch.append(vmem((2,) * (steps - 1 - s) + (rows // 2, cols), BF16))
    qkv_grad, out_grad, gain = pl.pallas_call(
        functools.partial(kernel, plan),
        out_shape=(
            jax.ShapeDtypeStruct((rows, 3 * width), F32),
            jax.ShapeDtypeStruct((rows, width), F32),
            jax.ShapeDtypeStruct((plan.n, 8, rows), F32),
        ),
        in_specs=[pl.BlockSpec(memory_space=pltpu.VMEM)] * 9,
        out_specs=[pl.BlockSpec(memory_space=pltpu.VMEM)] * 3,
        scratch_shapes=scratch,
        compiler_params=pltpu.CompilerParams(
            collective_id=0, has_side_effects=True, vmem_limit_bytes=58 * 2**20
        ),
    )(
        patches.reshape(flat), cotangent.reshape(flat), live, bias, norm_gain[None], qkv_weight,
        out_weight, signs_qkv[None], signs_out[None],
    )
    return qkv_grad, out_grad, gain[:, 0].reshape(width) / norm_gain


def solution(mesh):
    def device(patches, cotangent, segment_ids, live_packs, norm_gain, qkv_weight, *others):
        packs, length, width = patches.shape
        plan = Plan(
            mesh.shape["outer"], mesh.shape["inner"], packs, length, width, qkv_weight.shape[0]
        )
        return on_device(
            plan, patches, cotangent, segment_ids, live_packs, norm_gain, qkv_weight, *others
        )

    return jax.shard_map(
        device,
        mesh=mesh,
        in_specs=(
            P(("outer", "inner"), None, None),
            P(("outer", "inner"), None, None),
            P(("outer", "inner"), None),
            P(("outer", "inner")),
            P(),
            P("inner", None),
            P("inner", None),
            P(),
            P(),
        ),
        out_specs=(P("inner", None), P("inner", None), P()),
        check_vma=False,
    )
```

```python
import functools

import jax
import jax.numpy as jnp
from jax import lax
from jax.experimental import pallas as pl
from jax.experimental.pallas import tpu as pltpu
from jax.sharding import PartitionSpec as P

HEAD_DIM = 64
EPSILON = 1e-06
CLIP_RATIO = 2.0
BLOCK = 128
BLOCK_SCALE = 0.08838834764831845
GROUP = 256
F32 = jnp.float32
BF16 = jnp.bfloat16
MESH = pl.DeviceIdType.MESH


def dot_nn(a, b):
    return lax.dot_general(a, b, (((1,), (0,)), ((), ())), preferred_element_type=F32)


def dot_nt(a, b):
    return lax.dot_general(a, b, (((1,), (1,)), ((), ())), preferred_element_type=F32)


def dot_tn(a, b):
    return lax.dot_general(a, b, (((0,), (0,)), ((), ())), preferred_element_type=F32)


def hadamard():
    rows = lax.broadcasted_iota(jnp.int32, (BLOCK, BLOCK), 0)
    cols = lax.broadcasted_iota(jnp.int32, (BLOCK, BLOCK), 1)
    common = rows & cols
    total = jnp.zeros_like(common)
    for level in range(7):
        total = total + ((common >> level) & 1)
    return (1 - 2 * (total & 1)).astype(F32).astype(BF16)


def turn(block, table):
    high = block.astype(BF16)
    low = (block - high.astype(F32)).astype(BF16)
    return (dot_nn(high, table) + dot_nn(low, table)) * BLOCK_SCALE


class Plan:
    def __init__(self, n_outer, n_inner, packs, length, width, rows):
        self.no, self.n = n_outer, n_inner
        self.bits = n_inner.bit_length() - 1
        self.packs, self.length, self.width, self.rows = packs, length, width, rows
        self.total = packs * length
        self.groups = width // GROUP
        self.share = rows // n_outer
        self.wire = BF16 if self.share % 16 == 0 else F32
        self.chunks = self.groups + 1
        self.cols = [3 * GROUP] * self.groups + [width]
        upper = list(range(self.bits - 1))
        self.orders = [upper[::-1], upper]
        per_gather = 2 * self.bits
        per_scatter = 1 + 2 * (self.bits - 1)
        per_outer = 2 * (self.no - 1)
        self.messages = (
            self.chunks * (per_gather + per_scatter + per_outer) + (self.no - 1) + self.bits
        )


def kernel(plan, x_ref, cot_ref, live_ref, bias_ref, gain_ref, wq_ref, wo_ref, sq_ref, so_ref,
           oq_ref, oo_ref, og_ref, *scratch):
    names = list(scratch)

    def take(count):
        got = names[:count]
        del names[:count]
        return got

    send_sem, recv_sem, hid, hid_t, cot, proj, gatt, att_t, gproj, gacc, gpart, gall = take(12)
    ch = plan.chunks
    weights, grads, from_twin, sums = take(ch), take(ch), take(ch), take(ch)
    clipped, from_outer, decoded = take(ch), take(ch), take(ch)
    steps = plan.bits - 1
    got_half = [[take(steps) for _ in range(2)] for _ in range(ch)]
    sum_half = [[take(steps - 1) for _ in range(2)] for _ in range(ch)]

    outer, inner = lax.axis_index("outer"), lax.axis_index("inner")
    bits, rows, length, no = plan.bits, plan.rows, plan.length, plan.no
    half = rows // 2
    stride = [2 ** (bits - 1 - b) for b in range(bits)]
    mine = [lax.rem(inner // stride[b], 2) for b in range(bits)]
    partner = [inner + (1 - 2 * mine[b]) * stride[b] for b in range(bits)]
    counter = [0]

    barrier = pltpu.get_barrier_semaphore()
    for b in range(bits):
        pl.semaphore_signal(barrier, inc=1, device_id={"inner": partner[b]}, device_id_type=MESH)
    for j in range(1, no):
        pl.semaphore_signal(
            barrier, inc=1, device_id={"outer": lax.rem(outer + j, no)}, device_id_type=MESH
        )

    def message(src, dst, where):
        at = counter[0]
        counter[0] += 1
        return pltpu.make_async_remote_copy(
            src_ref=src, dst_ref=dst, send_sem=send_sem.at[at], recv_sem=recv_sem.at[at],
            device_id=where, device_id_type=MESH,
        )

    started = []

    def launch(messages):
        for one in messages:
            one.start()
            started.append(one)

    def arrive(messages):
        for one in messages:
            one.wait_recv()

    gathers = []
    for k in range(ch):
        levels = []
        for s in range(bits):
            level = []
            for h in range(2):
                order = plan.orders[h] + [bits - 1]
                spot = tuple(
                    slice(None) if b in order[:s] else mine[b] for b in range(bits)
                ) + (pl.ds(h * half, half),)
                ref = weights[k].at[spot]
                level.append(message(ref, ref, {"inner": partner[order[s]]}))
            levels.append(level)
        gathers.append(levels)

    def gather(k, s):
        if s > 0:
            arrive(gathers[k][s - 1])
        launch(gathers[k][s])

    own = tuple(mine)
    out = plan.groups
    weights[out][own] = wo_ref[...]
    for g in range(plan.groups):
        for part in range(3):
            at = part * plan.width + g * GROUP
            weights[g][own + (slice(None), pl.ds(part * GROUP, GROUP))] = wq_ref[:, at:at + GROUP]
    pl.semaphore_wait(barrier, bits + no - 1)

    gather_order = [out] + list(range(plan.groups))
    gather(out, 0)
    gather(0, 0)
    gather(1, 0)

    def norm_pack(p):
        at = pl.ds(pl.multiple_of(p * length, length), length)
        inputs = x_ref[at, :].astype(F32)
        center = inputs - jnp.mean(inputs, axis=-1, keepdims=True)
        spread = jnp.mean(center * center, axis=-1, keepdims=True)
        value = center * lax.rsqrt(spread + EPSILON) * gain_ref[...]
        hid[at, :] = value.astype(BF16)
        hid_t[:, at] = value.T.astype(BF16)
        cot[at, :] = (cot_ref[at, :].astype(F32) * live_ref[p][0:1, 0:1]).astype(BF16)

    pl.loop(0, plan.packs // 2)(norm_pack)
    gather(out, 1)
    gather(0, 1)
    pl.loop(plan.packs // 2, plan.packs)(norm_pack)
    for k in range(2, plan.groups):
        gather(k, 0)
    gather(out, 2)
    gather(1, 1)
    gather(0, 2)
    arrive(gathers[out][bits - 1]) if bits == 3 else None

    table = hadamard()

    pending = []
    if bits != 3:
        for k in (out, 0):
            for s in range(3, bits):
                pending.append((k, s))
    for k in range(1, plan.groups):
        for s in range(bits):
            if s > 0 and (k, s) != (1, 1):
                pending.append((k, s))

    def gather_upto(k):
        while any(entry[0] == k for entry in pending):
            gather(*pending.pop(0))

    if bits != 3:
        gather_upto(out)
        gather_upto(0)
        arrive(gathers[out][bits - 1])

    taken = bits - (GROUP // rows).bit_length() + 1

    def grad_att(g):
        spot = tuple((g >> (taken - 1 - b)) & 1 for b in range(taken))
        block = weights[out][spot].reshape(GROUP, plan.width)
        gatt[:, g * GROUP:(g + 1) * GROUP] = dot_nt(cot[...], block).astype(BF16)

    for g in range(plan.groups):
        grad_att(g)

    def project(g):
        arrive(gathers[g][bits - 1])
        for part in range(3):
            cols = pl.ds(part * GROUP, GROUP)
            block = weights[g][(slice(None),) * (bits + 1) + (cols,)]
            proj[:, cols] = dot_nn(hid[...], block.reshape(plan.width, GROUP)).astype(BF16)

    lane = lax.broadcasted_iota(jnp.int32, (length, BLOCK), 1)
    first = lane < HEAD_DIM

    def stack(value):
        zero = jnp.zeros_like(value)
        return jnp.concatenate([jnp.where(first, value, zero), jnp.where(first, zero, value)], 0)

    paired = 2 if plan.packs % 2 == 0 else 1

    def attend(g):
        def one(p, j):
            at = pl.ds(pl.multiple_of(p * length, length), length)
            bias = bias_ref[p]
            bias = jnp.concatenate([bias, bias], 1)
            cols = [pl.ds(part * GROUP + j * BLOCK, BLOCK) for part in range(3)]
            query, key, value = (proj[at, c] for c in cols)
            spot = g * GROUP + j * BLOCK
            queries = stack(query)
            scores = dot_nt(key, queries) * (HEAD_DIM ** -0.5) + bias
            power = jnp.exp(scores - jnp.max(scores, axis=0, keepdims=True))
            prob = power * (1.0 / jnp.sum(power, axis=0, keepdims=True))
            rounded = prob.astype(BF16)
            mixed = dot_tn(value, rounded).astype(BF16)
            att_t[spot:spot + HEAD_DIM, at] = mixed[:HEAD_DIM, :length]
            att_t[spot + HEAD_DIM:spot + BLOCK, at] = mixed[HEAD_DIM:, length:]
            grads_out = stack(gatt[at, spot:spot + BLOCK])
            grad_prob = dot_nt(value, grads_out).astype(BF16).astype(F32)
            inside = jnp.sum(grad_prob * prob, axis=0, keepdims=True)
            grad_score = (prob * (grad_prob - inside) * (HEAD_DIM ** -0.5)).astype(BF16)
            turned = dot_tn(key, grad_score)
            turned = jnp.concatenate([turned[:HEAD_DIM, :length], turned[HEAD_DIM:, length:]], 0)
            gproj[at, cols[0]] = turned.T.astype(BF16)
            gproj[at, cols[1]] = dot_nn(grad_score, queries).astype(BF16)
            gproj[at, cols[2]] = dot_nn(rounded, grads_out).astype(BF16)

        @pl.loop(0, plan.packs // paired)
        def _(step):
            for e in range(paired):
                for j in range(GROUP // BLOCK):
                    one(step * paired + e, j)

    def block_spot(i):
        return tuple((i >> (bits - 1 - b)) & 1 for b in range(bits))

    def weight_grad(k, left, right):
        tall = max(rows, GROUP)
        per = tall // rows
        for i in range(0, plan.n, per):
            product = dot_nn(left[i * rows:i * rows + tall, :], right[...]).astype(BF16)
            for e in range(per):
                grads[k][block_spot(i + e)] = product[e * rows:(e + 1) * rows]

    last = bits - 1
    live = {}

    def add(a, b):
        return a.astype(F32) + b.astype(F32)

    def stage_twin(k):
        spot = (slice(None),) * last
        msg = message(grads[k].at[spot + (1 - mine[last],)], from_twin[k], {"inner": partner[last]})
        launch([msg])
        live[k] = [msg]

    def stage_half(k, s):
        arrive(live[k])
        messages = []
        if s == 0:
            sums[k][...] = add(
                grads[k][(slice(None),) * last + (mine[last],)], from_twin[k][...]
            ).astype(BF16)
        finals = []
        for h in range(2):
            order = plan.orders[h][::-1]
            if s == 0:
                source, remaining = sums[k], list(range(last))
                tail = (pl.ds(h * half, half),)
            else:
                remaining = [b for b in range(last) if b not in order[:s - 1]]
                before = sums[k] if s == 1 else sum_half[k][h][s - 2]
                tail = (pl.ds(h * half, half),) if s == 1 else ()
                spot = tuple(
                    mine[b] if b == order[s - 1] else slice(None) for b in remaining
                ) + tail
                value = add(before[spot], got_half[k][h][s - 1][...])
                remaining = [b for b in remaining if b != order[s - 1]]
                if s == steps:
                    finals.append(value)
                    continue
                sum_half[k][h][s - 1][...] = value.astype(BF16)
                source, tail = sum_half[k][h][s - 1], ()
            spot = tuple(
                1 - mine[b] if b == order[s] else slice(None) for b in remaining
            ) + tail
            messages.append(message(
                source.at[spot], got_half[k][h][s], {"inner": partner[order[s]]}
            ))
        if s < steps:
            launch(messages)
            live[k] = messages
            return
        stage_clip(k, finals)

    def signs_at(k, b):
        if k == out:
            at, ref = b * BLOCK, so_ref
        else:
            per = GROUP // BLOCK
            at, ref = (b // per) * plan.width + k * GROUP + (b % per) * BLOCK, sq_ref
        return at, (1 - 2 * ref[:, at:at + BLOCK]).astype(F32)

    def stage_clip(k, finals):
        whole = jnp.concatenate(finals, 0)
        partial = None
        for b in range(plan.cols[k] // BLOCK):
            block = whole[:, b * BLOCK:(b + 1) * BLOCK]
            at, signs = signs_at(k, b)
            if k != out:
                term = block * wq_ref[:, at:at + BLOCK].astype(F32)
                partial = term if partial is None else partial + term
            value = turn(block * signs, table)
            bound = CLIP_RATIO * jnp.sqrt(
                jnp.mean(value * value, axis=-1, keepdims=True) + EPSILON
            )
            value = jnp.clip(value, -bound, bound)
            clipped[k][:, :, b * BLOCK:(b + 1) * BLOCK] = value.reshape(
                no, plan.share, BLOCK
            ).astype(plan.wire)
        if k != out:
            gacc[...] = partial if k == 0 else gacc[...] + partial
        messages = []
        for j in range(1, no):
            there = lax.rem(outer + j, no)
            messages.append(message(
                clipped[k].at[there], from_outer[k].at[j - 1], {"outer": there}
            ))
        launch(messages)
        live[k] = messages

    def stage_decode(k):
        arrive(live[k])
        total = clipped[k][outer].astype(F32)
        for j in range(1, no):
            total = total + from_outer[k][j - 1].astype(F32)
        for b in range(plan.cols[k] // BLOCK):
            signs = signs_at(k, b)[1]
            value = turn(total[:, b * BLOCK:(b + 1) * BLOCK], table) * signs
            decoded[k][outer, :, b * BLOCK:(b + 1) * BLOCK] = value.astype(plan.wire)
        messages = []
        for j in range(1, no):
            ref = decoded[k].at[outer]
            messages.append(message(ref, ref, {"outer": lax.rem(outer + j, no)}))
        launch(messages)
        live[k] = messages

    def stage_store(k):
        arrive(live[k])
        for part in range(1 if k == out else 3):
            wide = plan.width if k == out else GROUP
            value = decoded[k][:, :, part * wide:(part + 1) * wide].astype(F32)
            value = value.reshape(rows, wide)
            if k == out:
                oo_ref[...] = value
            else:
                at = part * plan.width + k * GROUP
                oq_ref[:, at:at + GROUP] = value

    def stages(k):
        todo = [functools.partial(stage_half, k, s) for s in range(steps + 1)]
        return todo + [functools.partial(stage_decode, k), functools.partial(stage_store, k)]

    queues = []

    def advance():
        for queue in queues:
            if queue:
                queue.pop(0)()

    for g in range(plan.groups):
        gather_upto(g)
        project(g)
        if g + 1 < plan.groups:
            while pending and pending[0][0] <= g + 1:
                gather(*pending.pop(0))
        if pending:
            gather(*pending.pop(0))
        advance()
        attend(g)
        for _ in range(min(2, len(pending))):
            gather(*pending.pop(0))
        advance()
        weight_grad(g, hid_t, gproj)
        stage_twin(g)
        queues.append(stages(g))
        if pending:
            gather(*pending.pop(0))
        advance() if g > 0 else None

    weight_grad(out, att_t, cot)
    stage_twin(out)
    queues.append(stages(out))
    while len(queues[out - 1]) > 2:
        advance()

    ones = jnp.ones((8, BLOCK), F32)
    gpart[outer] = lax.dot_general(
        ones, gacc[...], (((1,), (1,)), ((), ())), precision=lax.Precision.HIGHEST,
        preferred_element_type=F32,
    )
    gain_messages = []
    for j in range(1, no):
        ref = gpart.at[outer]
        gain_messages.append(message(ref, ref, {"outer": lax.rem(outer + j, no)}))
    launch(gain_messages)
    advance()
    arrive(gain_messages)
    total = gpart[0]
    for j in range(1, no):
        total = total + gpart[j]
    gall[own] = total
    for b in range(bits):
        spot = tuple(slice(None) if e < b else mine[e] for e in range(bits))
        ref = gall.at[spot]
        step = message(ref, ref, {"inner": partner[b]})
        launch([step])
        if b < 2:
            advance()
        arrive([step])
    for i in range(plan.n):
        og_ref[i] = gall[block_spot(i)]
    while any(queues):
        advance()
    for one in started:
        one.wait_send()


def on_device(plan, patches, cotangent, segment_ids, live_packs, norm_gain, qkv_weight, out_weight,
              signs_qkv, signs_out):
    width, rows, no = plan.width, plan.rows, plan.no
    flat = (plan.total, width)
    live = (jnp.arange(plan.packs, dtype=jnp.int32) < live_packs[0]).astype(F32)
    live = jnp.broadcast_to(live[:, None, None], (plan.packs, 8, BLOCK))
    allowed = segment_ids[:, :, None] == segment_ids[:, None, :]
    bias = jnp.where(allowed, 0.0, -1e30).astype(F32)
    two = (2,) * plan.bits
    vmem = pltpu.VMEM
    scratch = [
        pltpu.SemaphoreType.DMA((plan.messages,)),
        pltpu.SemaphoreType.DMA((plan.messages,)),
        vmem(flat, BF16),
        vmem(flat[::-1], BF16),
        vmem(flat, BF16),
        vmem((plan.total, 3 * GROUP), BF16),
        vmem(flat, BF16),
        vmem(flat[::-1], BF16),
        vmem((plan.total, 3 * GROUP), BF16),
        vmem((rows, BLOCK), F32),
        vmem((no, 8, rows), F32),
        vmem(two + (8, rows), F32),
    ]
    for shape, kind in (
        (two + (rows,), BF16), (two + (rows,), BF16), (two[1:] + (rows,), BF16),
        (two[1:] + (rows,), BF16), ((no, plan.share), plan.wire),
        ((no - 1, plan.share), plan.wire), ((no, plan.share), plan.wire),
    ):
        scratch += [vmem(shape + (cols,), kind) for cols in plan.cols]
    steps = plan.bits - 1
    for count in (steps, steps - 1):
        for cols in plan.cols:
            for _ in range(2):
                for s in range(count):
                    scratch.append(vmem((2,) * (steps - 1 - s) + (rows // 2, cols), BF16))
    qkv_grad, out_grad, gain = pl.pallas_call(
        functools.partial(kernel, plan),
        out_shape=(
            jax.ShapeDtypeStruct((rows, 3 * width), F32),
            jax.ShapeDtypeStruct((rows, width), F32),
            jax.ShapeDtypeStruct((plan.n, 8, rows), F32),
        ),
        in_specs=[pl.BlockSpec(memory_space=pltpu.VMEM)] * 9,
        out_specs=[pl.BlockSpec(memory_space=pltpu.VMEM)] * 3,
        scratch_shapes=scratch,
        compiler_params=pltpu.CompilerParams(
            collective_id=0, has_side_effects=True, vmem_limit_bytes=58 * 2**20
        ),
    )(
        patches.reshape(flat), cotangent.reshape(flat), live, bias, norm_gain[None], qkv_weight,
        out_weight, signs_qkv[None], signs_out[None],
    )
    return qkv_grad, out_grad, gain[:, 0].reshape(width) / norm_gain


def solution(mesh):
    def device(patches, cotangent, segment_ids, live_packs, norm_gain, qkv_weight, *others):
        packs, length, width = patches.shape
        plan = Plan(
            mesh.shape["outer"], mesh.shape["inner"], packs, length, width, qkv_weight.shape[0]
        )
        return on_device(
            plan, patches, cotangent, segment_ids, live_packs, norm_gain, qkv_weight, *others
        )

    return jax.shard_map(
        device,
        mesh=mesh,
        in_specs=(
            P(("outer", "inner"), None, None),
            P(("outer", "inner"), None, None),
            P(("outer", "inner"), None),
            P(("outer", "inner")),
            P(),
            P("inner", None),
            P("inner", None),
            P(),
            P(),
        ),
        out_specs=(P("inner", None), P("inner", None), P()),
        check_vma=False,
    )
```
